128 devices in a mesh: lat: 32 (over z, x, core), lon: 4 (over y).
Axes of the slice: x: 4, y: 4, z: 4, core: 2. Of those that a mesh axis runs over, the one named last changes fastest.
Arguments:
- grid_latent: bfloat16 [262144, 256], P(('lat', 'lon')), may hold values from -6 to 6
- mesh_latent: bfloat16 [32768, 256], P(('lat', 'lon')), may hold values from -6 to 6
- encode_sends: int32 [384, 4, 128], P(('lat', 'lon')), may hold values from 0 to 2047
- encode_sources: int32 [524288], P(('lat', 'lon')), may hold values from 0 to 1535, as said below
- encode_targets: int32 [524288], P(('lat', 'lon')), may hold values from 0 to 256, as said below
- mesh_sources: int32 [262144], P(('lat', 'lon')), may hold values from 0 to 2303, as said below
- mesh_targets: int32 [262144], P(('lat', 'lon')), may hold values from 0 to 256, as said below
- decode_sources: int32 [262144, 3], P(('lat', 'lon')), may hold values from 0 to 3071, as said below
- encode_weights: bfloat16 [4, 256, 256], replicated, may hold values from -0.375 to 0.375
- process_weights: bfloat16 [8, 256, 256], replicated, may hold values from -0.375 to 0.375
- decode_weights: bfloat16 [4, 256, 256], replicated, may hold values from -0.375 to 0.375
- norm_gains: bfloat16 [4, 256], replicated, may hold values from 0.099609375 to 1.8984375
Outputs:
- grid_out: bfloat16 [262144, 256], P(('lat', 'lon'))
- mesh_out: bfloat16 [32768, 256], P(('lat', 'lon'))
The draws below stay inside these ranges and needn't reach their ends.
Inputs may be any that keep to these rules, and one draw needn't show every extreme that they name: `encode_sources`: rows of encode_rows: a device of the first band uses none from the band below, one of the last band none from the band above. `encode_targets`: per device, 4096 edge slots; 256 marks padding, which comes after all live edges; devices of the first and last bands have no padding. `mesh_sources`: rows of the neighbourhood: a device of the first band uses none from the band below, one of the last band none from the band above. `mesh_targets`: per device, 2048 edge slots; 256 marks padding, which comes after all live edges; devices of the first and last bands have no padding. `decode_sources`: rows of band_table: a device of the first band uses none from the band below, one of the last band none from the band above.
All inputs are finite; a program needn't handle non-finite values.
Results may differ from the reference program's by a relative error of at most 0.013.
Values may be sent and summed in bfloat16 or wider, within the bound.
No kernel may reach another device: no remote copies, remote signals or barrier semaphores. Data moves between devices by JAX's collectives and lax.ppermute only.
A program may use at most 64 MiB of HBM per device.

```python
from functools import partial
import jax
import jax.numpy as jnp
from jax import lax

L = 256
G_DEV = 2048
M_DEV = 256
STEPS = 2
CAP_G = 128
E_G2M = 4096
E_MESH = 2048
GRID = 262144
MESH = 32768
N_LAT = 32
N_LON = 4
DEVICES = 128


def offset_rows(key, per_device, inner, row_count):
    first, second = jax.random.split(key)
    device = jnp.arange(row_count, dtype=jnp.int32) // per_device
    band_index = device // N_LON
    offset = jax.random.randint(first, (row_count,), 0, 3)
    offset = jnp.where((band_index == 0) & (offset == 0), 1, offset)
    offset = jnp.where((band_index == N_LAT - 1) & (offset == 2), 1, offset)
    position = jax.random.randint(second, (row_count,), 0, inner)
    return (offset * inner + position).astype(jnp.int32)


def live_targets(key, per_device, node_count):
    first, second = jax.random.split(key)
    row_count = DEVICES * per_device
    device = jnp.arange(row_count, dtype=jnp.int32) // per_device
    edge_slot = jnp.arange(row_count, dtype=jnp.int32) % per_device
    band_index = jnp.arange(DEVICES, dtype=jnp.int32) // N_LON
    distance = jnp.minimum(band_index, N_LAT - 1 - band_index)
    half_bands = max(N_LAT // 2, 1)
    jitter = jax.random.randint(first, (DEVICES,), 0, per_device // 8 + 1)
    live_count = per_device - per_device // 2 * distance // half_bands - jnp.where(distance > 0, jitter, 0)
    target = jax.random.randint(second, (row_count,), 0, node_count)
    return jnp.where(edge_slot < live_count[device], target, node_count).astype(jnp.int32)


def draw_encode_sources(key, part):
    key = jax.random.fold_in(key, 11)
    return offset_rows(key, E_G2M, N_LON * CAP_G, DEVICES * E_G2M)


def draw_encode_targets(key, part):
    key = jax.random.fold_in(key, 12)
    return live_targets(key, E_G2M, M_DEV)


def draw_mesh_sources(key, part):
    key = jax.random.fold_in(key, 13)
    return offset_rows(key, E_MESH, 3 * M_DEV, DEVICES * E_MESH)


def draw_mesh_targets(key, part):
    key = jax.random.fold_in(key, 14)
    return live_targets(key, E_MESH, M_DEV)


def draw_decode_sources(key, part):
    key = jax.random.fold_in(key, 15)
    return offset_rows(key, 3 * G_DEV, N_LON * M_DEV, GRID * 3).reshape(GRID, 3)


def place_ends(result, key, low, largest):
    index_at = [jax.random.randint(jax.random.fold_in(key, axis), (), 0, length) for axis, length in enumerate(result.shape)]
    widest = result.shape.index(max(result.shape))
    beside = index_at[:widest] + [(index_at[widest] + 1) % result.shape[widest]] + index_at[widest + 1:]
    return result.at[tuple(index_at)].set(low).at[tuple(beside)].set(largest)


def block_levels(stream_key, dims, shards, smallest, high):
    loudness, own = 1.0, jax.random.fold_in(stream_key, 6)
    for dim, blocks in shards:
        draws = jnp.exp(jax.random.uniform(jax.random.fold_in(own, dim), (blocks,), jnp.float32, smallest / len(shards), high / len(shards)))
        loudness = loudness * jnp.repeat(draws, dims[dim] // blocks).reshape([-1 if axis == dim else 1 for axis in range(len(dims))])
    return loudness


def bell_draw(key, shape, deviation, most, cuts=(), kind=jnp.bfloat16):
    values = deviation * jax.random.normal(key, shape, jnp.float32)
    if cuts:
        values = values * block_levels(key, shape, cuts, -0.22, 0.18)
    return jnp.clip(values, -most, most).astype(kind)


def setup_inputs(seed: int = 0) -> dict:
    arg_keys = jax.random.split(jax.random.key(seed), 13)
    return {
        "grid_latent": bell_draw(arg_keys[0], (GRID, L), 1.0, 6.0, ((0, 128),)),
        "mesh_latent": bell_draw(arg_keys[1], (MESH, L), 1.0, 6.0, ((0, 128),)),
        "encode_sends": place_ends(jax.random.randint(arg_keys[2], (3 * DEVICES, N_LON, CAP_G), 0, G_DEV), jax.random.fold_in(arg_keys[2], 1), 0, G_DEV - 1).astype(jnp.int32),
        "encode_sources": draw_encode_sources(jax.random.fold_in(arg_keys[12], 71), 0),
        "encode_targets": draw_encode_targets(jax.random.fold_in(arg_keys[12], 71), 0),
        "mesh_sources": draw_mesh_sources(jax.random.fold_in(arg_keys[12], 71), 0),
        "mesh_targets": draw_mesh_targets(jax.random.fold_in(arg_keys[12], 71), 0),
        "decode_sources": draw_decode_sources(jax.random.fold_in(arg_keys[12], 71), 0),
        "encode_weights": bell_draw(arg_keys[8], (4, L, L), L ** -0.5, 0.375),
        "process_weights": bell_draw(arg_keys[9], (4 * STEPS, L, L), L ** -0.5, 0.375),
        "decode_weights": bell_draw(arg_keys[10], (4, L, L), L ** -0.5, 0.375),
        "norm_gains": jnp.clip(1.0 + 0.18 * jax.random.normal(arg_keys[11], (STEPS + 2, L), jnp.float32), 0.099609375, 1.8984375).astype(jnp.bfloat16),
    }


epsilon = 1e-05

def project(source_rows, weight):
    return jnp.dot(source_rows, weight, preferred_element_type=jnp.float32).astype(jnp.bfloat16)

def node_update(latent, summed, gain_row, node_weight):
    mean_square = lax.optimization_barrier(jnp.mean(summed * summed, axis=-1, keepdims=True))
    scaled = (summed * lax.rsqrt(mean_square + epsilon) * gain_row.astype(jnp.float32)).astype(jnp.bfloat16)
    return (latent.astype(jnp.float32) + jnp.dot(scaled, node_weight, preferred_element_type=jnp.float32)).astype(jnp.bfloat16)

def edge_sums(source_rows, target_proj, sources, targets, edge_weight):
    node_count = target_proj.shape[0]
    picked = jnp.take(source_rows, sources, axis=0).astype(jnp.float32)
    target_rows = jnp.take(target_proj, jnp.minimum(targets, node_count - 1), axis=0)
    hidden = jax.nn.silu(picked + target_rows).astype(jnp.bfloat16)
    message = jnp.dot(hidden, edge_weight, preferred_element_type=jnp.float32).astype(jnp.bfloat16)
    summed = jax.ops.segment_sum(message.astype(jnp.float32), targets, num_segments=node_count + 1)
    return summed[:node_count]

def band_shift(blocks, offset):
    filler = jnp.zeros_like(blocks[:1])
    if offset == -1:
        return jnp.concatenate([filler, blocks[:-1]], 0)
    if offset == 1:
        return jnp.concatenate([blocks[1:], filler], 0)
    return blocks

def take_rows(table, indices):
    return jnp.take(table, indices, axis=0)

def encode_one(weights, gain_row, packed):
    source_rows, latent, sources, targets = packed
    target_proj = jnp.dot(latent, weights[1], preferred_element_type=jnp.float32)
    summed = edge_sums(source_rows, target_proj, sources, targets, weights[2])
    return node_update(latent, summed, gain_row, weights[3])

def mesh_step(weights, gain_row, packed):
    halo_rows, latent, sources, targets = packed
    target_proj = jnp.dot(latent, weights[1], preferred_element_type=jnp.float32)
    summed = edge_sums(halo_rows, target_proj, sources, targets, weights[2])
    return node_update(latent, summed, gain_row, weights[3])

def decode_one(weights, gain_row, packed):
    near_rows, grid_rows, sources = packed
    grid_proj = jnp.dot(grid_rows, weights[1], preferred_element_type=jnp.float32)
    picked = jnp.take(near_rows, sources.reshape(-1), axis=0).astype(jnp.float32).reshape(sources.shape[0], 3, grid_rows.shape[1])
    hidden = jax.nn.silu(picked + grid_proj[:, None, :]).astype(jnp.bfloat16)
    message = jnp.dot(hidden.reshape(-1, grid_rows.shape[1]), weights[2], preferred_element_type=jnp.float32).astype(jnp.bfloat16)
    summed = lax.optimization_barrier(jnp.sum(message.astype(jnp.float32).reshape(sources.shape[0], 3, grid_rows.shape[1]), axis=1))
    return node_update(grid_rows, summed, gain_row, weights[3])

def reference(grid_latent, mesh_latent, encode_sends, encode_sources, encode_targets, mesh_sources, mesh_targets, decode_sources, encode_weights, process_weights, decode_weights, norm_gains):
    grid_table = project(grid_latent, encode_weights[0]).reshape(N_LAT, N_LON, G_DEV, L)
    send_lists = encode_sends.reshape(N_LAT, N_LON, 3, N_LON, CAP_G)
    pieces = []
    for offset in range(3):
        table_there = band_shift(grid_table, offset - 1)
        index_there = band_shift(send_lists[:, :, 2 - offset], offset - 1)
        pieces.append(jax.vmap(jax.vmap(take_rows))(table_there, index_there))
    arrived = jnp.stack(pieces, 0).transpose(1, 3, 0, 2, 4, 5).reshape(DEVICES, 3 * N_LON * CAP_G, L)
    mesh_now = lax.map(partial(encode_one, encode_weights, norm_gains[0]), (arrived, mesh_latent.reshape(DEVICES, M_DEV, L), encode_sources.reshape(DEVICES, E_G2M), encode_targets.reshape(DEVICES, E_G2M)))
    edge_sources = mesh_sources.reshape(DEVICES, E_MESH)
    edge_targets = mesh_targets.reshape(DEVICES, E_MESH)
    for step_number in range(STEPS):
        weights_now = process_weights[4 * step_number:4 * step_number + 4]
        sent_rows = project(mesh_now.reshape(MESH, L), weights_now[0]).reshape(N_LAT, N_LON, M_DEV, L)
        around_rows = []
        for lat_offset in range(3):
            band_rows = band_shift(sent_rows, lat_offset - 1)
            for lon_offset in range(3):
                around_rows.append(jnp.roll(band_rows, 1 - lon_offset, axis=1))
        halo_rows = jnp.stack(around_rows, 2).reshape(DEVICES, 9 * M_DEV, L)
        mesh_now = lax.map(partial(mesh_step, weights_now, norm_gains[1 + step_number]), (halo_rows, mesh_now, edge_sources, edge_targets))
    shared = project(mesh_now.reshape(MESH, L), decode_weights[0]).reshape(N_LAT, N_LON * M_DEV, L)
    near_rows = jnp.stack([band_shift(shared, -1), shared, band_shift(shared, 1)], 1).reshape(N_LAT, 3 * N_LON * M_DEV, L)
    near_rows = jnp.repeat(near_rows, N_LON, axis=0)
    grid_out = lax.map(partial(decode_one, decode_weights, norm_gains[STEPS + 1]), (near_rows, grid_latent.reshape(DEVICES, G_DEV, L), decode_sources.reshape(DEVICES, G_DEV, 3)))
    return (grid_out.reshape(GRID, L), mesh_now.reshape(MESH, L))
```

```python
from functools import partial

import jax
import jax.numpy as jnp
from jax import lax
from jax.experimental import pallas as pl
from jax.experimental.pallas import tpu as pltpu
from jax.sharding import PartitionSpec as P

STEPS = 2
epsilon = 1e-05
VMEM = pl.BlockSpec(memory_space=pltpu.VMEM)
SMEM = pl.BlockSpec(memory_space=pltpu.SMEM)
params = pltpu.CompilerParams(vmem_limit_bytes=50 * 2**20)
f32, bf16 = jnp.float32, jnp.bfloat16


def dot(a, b):
    return jnp.dot(a, b, preferred_element_type=f32)


def silu(z):
    half = 0.5 * z
    return half + half * jnp.tanh(half)


def node_update(latent, summed, gain_row, node_weight):
    mean_square = jnp.mean(summed * summed, axis=-1, keepdims=True)
    scaled = (summed * lax.rsqrt(mean_square + epsilon) * gain_row).astype(bf16)
    return latent.astype(f32) + dot(scaled, node_weight)


def split_rows(x):
    return x.astype(f32).reshape(x.shape[0], 2, 128)


def pick_rows(table, out, read, start, count):
    rows = [table[read(start + u)] for u in range(count)]
    for u in range(count):
        out[start + u] = rows[u]


def lane_copies(row):
    return jnp.transpose(jnp.broadcast_to(row, (128, 128)))


def send_kernel(place, lists, grid, weight, chip_out, cross_out, own_out, table, picked):
    odd, lon = place[0], place[1]
    slots = 128
    table[...] = dot(grid[...], weight[...]).reshape(table.shape)
    for part, out in enumerate((chip_out, cross_out, own_out)):
        side = (2 - 2 * odd, 2 * odd, 1)[part]
        for k in range(4):
            first = (side * 4 + lax.rem(lon + k, 4)) * slots
            base = (part * 4 + k) * slots

            @pl.loop(0, slots // 32)
            def _(i):
                rows = [table[lists[first + i * 32 + u]] for u in range(32)]
                for u in range(32):
                    picked[base + i * 32 + u] = rows[u]

            out[k] = picked[base : base + slots].reshape(slots, 256).astype(bf16)


def edge_pass(table, picked, sources, target_rows, target_proj, rows_per_block):
    edges = target_rows.shape[0] * 128
    nodes = target_proj.shape[0]
    lanes = lax.broadcasted_iota(jnp.int32, (128, nodes), 1)
    node_ids = lax.broadcasted_iota(jnp.int32, (nodes, 128), 0)
    total = jnp.zeros((nodes, 256), f32)

    def block(j, total):
        start = pl.multiple_of(j * rows_per_block, rows_per_block)

        @pl.loop(0, rows_per_block // 32)
        def _(i):
            pick_rows(table, picked, lambda e: sources[e], start + i * 32, 32)

        gathered = picked[pl.ds(start, rows_per_block)].reshape(rows_per_block, 256)
        pointers, incidence = [], []
        for q in range(rows_per_block // 128):
            row = target_rows[pl.ds(j * (rows_per_block // 128) + q, 1), :]
            copies = lane_copies(row)
            pointers.append(
                (jnp.concatenate([copies] * (nodes // 128), 1) == lanes).astype(bf16)
            )
            incidence.append((node_ids == row).astype(bf16))
        z = gathered + dot(jnp.concatenate(pointers, 0), target_proj)
        return total + dot(jnp.concatenate(incidence, 1), silu(z).astype(bf16))

    return lax.fori_loop(0, edges // rows_per_block, block, total)


def mesh_kernel(fill, place, sources, targets, latent, gain, weights, next_weight, *rest):
    *parts, latent_out, sent_out, table, picked = rest
    fill(place, table, parts)
    target_proj = dot(latent[...], weights[1]).astype(bf16)
    hidden = edge_pass(table, picked, sources, targets, target_proj, 256)
    summed = dot(hidden.astype(bf16), weights[2])
    new = node_update(latent[...], summed, gain[...].astype(f32), weights[3]).astype(bf16)
    latent_out[...] = new
    sent_out[...] = dot(new, next_weight[...]).astype(bf16)


def fill_encode(place, table, parts):
    odd, lon = place[0], place[1]
    bands = (2 - 2 * odd, 2 * odd, 1)
    for k, part in enumerate(parts):
        column = lax.rem(lon + 4 - k, 4)
        for i in range(3):
            table[pl.ds((bands[i] * 4 + column) * 128, 128)] = split_rows(part[i])


def fill_halo(place, table, parts):
    odd = place[0]
    for band, part in zip((1, 2 - 2 * odd, 2 * odd), parts):
        for q in range(3):
            table[pl.ds((band * 3 + q) * 256, 256)] = split_rows(part[q])


def fill_bands(place, table, parts):
    odd, lon = place[0], place[1]
    for band, part in zip((1, 2 - 2 * odd, 2 * odd), parts):
        for k in range(4):
            column = lax.rem(lon + 4 - k, 4)
            table[pl.ds((band * 4 + column) * 256, 256)] = split_rows(part[k])


def decode_kernel(fill, place, sources, grid, gain, weights, *rest):
    *parts, out, table, picked = rest
    fill(place, table, parts)
    rows = 256

    @pl.loop(0, grid.shape[0] // rows)
    def _(j):
        start = pl.multiple_of(j * rows, rows)

        @pl.loop(0, rows // 16)
        def _(i):
            first = i * 16
            for k in range(3):
                got = [table[sources[3 * (start + first + u) + k]] for u in range(16)]
                for u in range(16):
                    picked[k, first + u] = got[u]

        latent = grid[pl.ds(start, rows), :]
        proj = dot(latent, weights[1])
        hidden = sum(silu(picked[k].reshape(rows, 256) + proj) for k in range(3))
        summed = dot(hidden.astype(bf16), weights[2])
        out[pl.ds(start, rows), :] = node_update(
            latent, summed, gain[...].astype(f32), weights[3]
        ).astype(bf16)


def shape(*dims, dtype=bf16):
    return jax.ShapeDtypeStruct(dims, dtype)


def call(kernel, specs, outs, scratch, cost):
    return pl.pallas_call(
        kernel,
        in_specs=specs,
        out_specs=tuple(VMEM for _ in outs),
        out_shape=tuple(outs),
        scratch_shapes=scratch,
        compiler_params=params,
        cost_estimate=pl.CostEstimate(flops=cost, bytes_accessed=2**20, transcendentals=0),
    )


def along(x, by):
    return lax.ppermute(x, "lon", [(i, (i + by) % 4) for i in range(4)])


def swap_chip(x):
    return lax.ppermute(x, "lat", [(i, i ^ 1) for i in range(32)])


def swap_cross(x):
    return lax.ppermute(x, "lat", [(i, ((i + 1) ^ 1) - 1) if 0 < i < 31 else (i, 31 - i) for i in range(32)])


def shards(
    grid_latent,
    mesh_latent,
    encode_sends,
    encode_sources,
    encode_targets,
    mesh_sources,
    mesh_targets,
    decode_sources,
    encode_weights,
    process_weights,
    decode_weights,
    norm_gains,
):
    grid_count, latent = grid_latent.shape
    nodes = mesh_latent.shape[0]
    place = jnp.stack([lax.axis_index("lat") % 2, lax.axis_index("lon")]).astype(jnp.int32)

    chip, cross, own = call(
        send_kernel,
        [SMEM, SMEM, VMEM, VMEM],
        [shape(4, 128, latent)] * 3,
        [pltpu.VMEM((grid_count, 2, 128), f32), pltpu.VMEM((1536, 2, 128), f32)],
        10**9,
    )(place, encode_sends.reshape(-1), grid_latent, encode_weights[0])
    stacked = jnp.stack([swap_chip(chip), swap_cross(cross), own])
    parts = [stacked[:, 0]] + [along(stacked[:, k], k) for k in (1, 2, 3)]

    def mesh_call(fill, rows, edges, part_count):
        return call(
            partial(mesh_kernel, fill),
            [SMEM, SMEM] + [VMEM] * (5 + part_count),
            [shape(nodes, latent)] * 2,
            [pltpu.VMEM((rows, 2, 128), f32), pltpu.VMEM((edges, 2, 128), f32)],
            10**9,
        )

    mesh_now, sent = mesh_call(fill_encode, 1536, 4096, 4)(
        place,
        encode_sources,
        encode_targets.reshape(-1, 128),
        mesh_latent,
        norm_gains[0:1],
        encode_weights,
        process_weights[0],
        *parts,
    )
    for step in range(STEPS):
        weights = process_weights[4 * step : 4 * step + 4]
        following = process_weights[4 * step + 4] if step + 1 < STEPS else decode_weights[0]
        around = jnp.stack([along(sent, 1), sent, along(sent, -1)])
        mesh_now, sent = mesh_call(fill_halo, 9 * nodes, mesh_sources.shape[0], 3)(
            place,
            mesh_sources,
            mesh_targets.reshape(-1, 128),
            mesh_now,
            norm_gains[1 + step : 2 + step],
            weights,
            following,
            around,
            swap_chip(around),
            swap_cross(around),
        )
    band = jnp.stack([sent] + [along(sent, k) for k in (1, 2, 3)])
    (grid_out,) = call(
        partial(decode_kernel, fill_bands),
        [SMEM, SMEM] + [VMEM] * 6,
        [shape(grid_count, latent)],
        [pltpu.VMEM((12 * nodes, 2, 128), f32), pltpu.VMEM((3, 256, 2, 128), f32)],
        10**9,
    )(
        place,
        decode_sources.reshape(-1),
        grid_latent,
        norm_gains[STEPS + 1 : STEPS + 2],
        decode_weights,
        band,
        swap_chip(band),
        swap_cross(band),
    )
    return grid_out, mesh_now


def solution(mesh):
    rows = P(("lat", "lon"), None)
    flat = P(("lat", "lon"))
    return jax.shard_map(
        shards,
        mesh=mesh,
        in_specs=(rows, rows, P(("lat", "lon"), None, None), flat, flat, flat, flat, rows, P(), P(), P(), P()),
        out_specs=(rows, rows),
        check_vma=False,
    )
```

```python
from functools import partial

import jax
import jax.numpy as jnp
from jax import lax
from jax.experimental import pallas as pl
from jax.experimental.pallas import tpu as pltpu
from jax.sharding import PartitionSpec as P

STEPS = 2
EDGE_BLOCK = 1024
GRID_BLOCK = 512
epsilon = 1e-05
VMEM = pl.BlockSpec(memory_space=pltpu.VMEM)
SMEM = pl.BlockSpec(memory_space=pltpu.SMEM)
params = pltpu.CompilerParams(vmem_limit_bytes=20 * 2**20)
f32, bf16, i16 = jnp.float32, jnp.bfloat16, jnp.int16


def dot(a, b):
    return jnp.dot(a, b, preferred_element_type=f32)


def silu(z):
    half = 0.5 * z
    return half + half * jnp.tanh(half)


def node_update(latent, summed, gain_row, node_weight):
    mean_square = jnp.mean(summed * summed, axis=-1, keepdims=True)
    scaled = (summed * lax.rsqrt(mean_square + epsilon) * gain_row).astype(bf16)
    return latent.astype(f32) + dot(scaled, node_weight)


def send_kernel(place, lists, grid, weights, out0, out1, out2, out3, table, picked):
    odd, lon = place[0], place[1]
    slots = 128
    table[...] = dot(grid[...], weights[0]).reshape(table.shape)
    for k, out in enumerate((out0, out1, out2, out3)):
        column = lax.rem(lon + k, 4)
        for part, side in enumerate((1, 2 - 2 * odd, 2 * odd)):
            base = (part * 4 + k) * slots
            first = (side * 4 + column) * slots

            @pl.loop(0, slots // 32)
            def _(i):
                rows = [table[lists[first + i * 32 + u]] for u in range(32)]
                for u in range(32):
                    picked[base + i * 32 + u] = rows[u]

            out[part] = picked[base : base + slots].reshape(slots, 256).astype(bf16)


def lane_copies(row):
    return jnp.transpose(jnp.broadcast_to(row, (128, 128))).astype(i16)


def lanes_kernel(indices, out):
    for q in range(indices.shape[0]):
        out[q * 128 : (q + 1) * 128, :] = lane_copies(indices[q : q + 1, :])


def edge_lanes_kernel(sources, targets, source_out, target_out, incidence_out):
    lanes_kernel(sources, source_out)
    lanes_kernel(targets, target_out)
    node_ids = lax.broadcasted_iota(jnp.int32, (incidence_out.shape[0], 128), 0)
    for q in range(targets.shape[0]):
        incidence_out[:, q * 128 : (q + 1) * 128] = (node_ids == targets[q : q + 1, :]).astype(bf16)


def pointers(copies, starts, width):
    lane = lax.broadcasted_iota(jnp.int32, (1, 128), 1)
    one, zero = jnp.ones((), bf16), jnp.zeros((), bf16)
    return jnp.concatenate(
        [
            jnp.where(copies == (lane + (start + offset)).astype(i16), one, zero)
            for start in starts
            for offset in range(0, width, 128)
        ],
        1,
    )


def received_starts(place, width):
    odd, lon = place[0], place[1]
    return [[(band * 4 + lax.rem(lon + 4 - k, 4)) * width for k in range(4)] for band in (1, 2 - 2 * odd, 2 * odd)]


def halo_starts(place, width):
    odd = place[0]
    return [[(band * 3 + q) * width for q in range(3)] for band in (1, 2 - 2 * odd, 2 * odd)]


def early_edges_kernel(starts, place, sources, targets, own, chip, latent, weights, out):
    width = own.shape[1]
    own_starts, chip_starts, _ = starts(place, width)
    target_proj = dot(latent[...], weights[1]).astype(bf16)
    tables = [x[...].reshape(-1, 256) for x in (own, chip)]
    size = min(EDGE_BLOCK, out.shape[0])
    for first in range(0, out.shape[0], size):
        here = slice(first, first + size)
        copies = sources[here, :]
        out[here, :] = (
            dot(pointers(targets[here, :], [0], 256), target_proj)
            + dot(pointers(copies, own_starts, width), tables[0])
            + dot(pointers(copies, chip_starts, width), tables[1])
        ).astype(bf16)


def late_edges_kernel(
    starts, place, sources, early, cross, incidence, latent, gain, weights, following, latent_out, sent_out, hidden
):
    width = cross.shape[1]
    cross_starts = starts(place, width)[2]
    table = cross[...].reshape(-1, 256)
    size = min(EDGE_BLOCK, hidden.shape[0])
    for first in range(0, hidden.shape[0], size):
        here = slice(first, first + size)
        z = early[here, :].astype(f32) + dot(pointers(sources[here, :], cross_starts, width), table)
        hidden[here, :] = silu(z).astype(bf16)
    summed = dot(incidence[...], hidden[...])
    summed = dot(summed.astype(bf16), weights[2])
    new = node_update(latent[...], summed, gain[...].astype(f32), weights[3]).astype(bf16)
    latent_out[...] = new
    sent_out[...] = dot(new, following[...]).astype(bf16)


def early_grid_kernel(place, sources, own, chip, out):
    width = own.shape[1]
    own_starts, chip_starts, _ = received_starts(place, width)
    tables = [x[...].reshape(-1, 256) for x in (own, chip)]

    @pl.loop(0, out.shape[0] // EDGE_BLOCK)
    def _(j):
        here = pl.ds(pl.multiple_of(j * EDGE_BLOCK, EDGE_BLOCK), EDGE_BLOCK)
        copies = sources[here, :]
        out[here, :] = (
            dot(pointers(copies, own_starts, width), tables[0]) + dot(pointers(copies, chip_starts, width), tables[1])
        ).astype(bf16)


def late_grid_kernel(place, sources, early, cross, grid, proj, gain, weights, out):
    width = cross.shape[1]
    cross_starts = received_starts(place, width)[2]
    table = cross[...].reshape(-1, 256)
    gains = gain[...].astype(f32)
    count = grid.shape[0]
    for first in range(0, count, GRID_BLOCK):
        here = slice(first, first + GRID_BLOCK)
        base = proj[here, :].astype(f32)
        hidden = jnp.zeros((GRID_BLOCK, 256), f32)
        for k in range(3):
            rows = slice(k * count + first, k * count + first + GRID_BLOCK)
            late = dot(pointers(sources[rows, :], cross_starts, width), table)
            hidden += silu(late + early[rows, :].astype(f32) + base)
        summed = dot(hidden.astype(bf16), weights[2])
        out[here, :] = node_update(grid[here, :], summed, gains, weights[3]).astype(bf16)


def project_kernel(rows, weights, out):
    out[...] = dot(rows[...], weights[1]).astype(bf16)


def shape(*dims, dtype=bf16):
    return jax.ShapeDtypeStruct(dims, dtype)


def call(kernel, specs, outs, scratch, cost):
    return pl.pallas_call(
        kernel,
        in_specs=specs,
        out_specs=tuple(VMEM for _ in outs),
        out_shape=tuple(outs),
        scratch_shapes=scratch,
        compiler_params=params,
        cost_estimate=pl.CostEstimate(flops=cost, bytes_accessed=2**20, transcendentals=0),
    )


def along(x, by):
    return lax.ppermute(x, "lon", [(i, (i + by) % 4) for i in range(4)])


def swap_chip(x):
    return lax.ppermute(x, "lat", [(i, i ^ 1) for i in range(32)])


def swap_cross(x):
    return lax.ppermute(x, "lat", [(i, ((i + 1) ^ 1) - 1) if 0 < i < 31 else (i, 31 - i) for i in range(32)])


def shards(
    grid_latent,
    mesh_latent,
    encode_sends,
    encode_sources,
    encode_targets,
    mesh_sources,
    mesh_targets,
    decode_sources,
    encode_weights,
    process_weights,
    decode_weights,
    norm_gains,
):
    grid_count, latent = grid_latent.shape
    nodes = mesh_latent.shape[0]
    place = jnp.stack([lax.axis_index("lat") % 2, lax.axis_index("lon")]).astype(jnp.int32)

    def edge_lanes(sources, targets):
        edges = sources.shape[0]
        return call(
            edge_lanes_kernel,
            [VMEM] * 2,
            [shape(edges, 128, dtype=i16)] * 2 + [shape(nodes, edges)],
            [],
            10**9,
        )(sources.reshape(-1, 128), targets.reshape(-1, 128))

    def edge_pass(starts, lanes, mesh_now, blocks, gain, weights, following):
        source_lanes, target_lanes, incidence = lanes
        edges = source_lanes.shape[0]
        chip, cross = swap_chip(blocks), swap_cross(blocks)
        rows = blocks.shape[0] * blocks.shape[1]
        (early,) = call(
            partial(early_edges_kernel, starts),
            [SMEM] + [VMEM] * 6,
            [shape(edges, latent)],
            [],
            2 * edges * 2 * rows * latent,
        )(place, source_lanes, target_lanes, blocks, chip, mesh_now, weights)
        return call(
            partial(late_edges_kernel, starts),
            [SMEM] + [VMEM] * 8,
            [shape(nodes, latent)] * 2,
            [pltpu.VMEM((edges, latent), bf16)],
            2 * edges * rows * latent,
        )(place, source_lanes, early, cross, incidence, mesh_now, gain, weights, following)

    outgoing = call(
        send_kernel,
        [SMEM, SMEM, VMEM, VMEM],
        [shape(3, 128, latent)] * 4,
        [pltpu.VMEM((grid_count, 2, 128), f32), pltpu.VMEM((1536, 2, 128), f32)],
        10**9,
    )(place, encode_sends.reshape(-1), grid_latent, encode_weights)
    encode_lanes = edge_lanes(encode_sources, encode_targets)
    mesh_lanes = edge_lanes(mesh_sources, mesh_targets)
    (grid_lanes,) = call(lanes_kernel, [VMEM], [shape(3 * grid_count, 128, dtype=i16)], [], 10**9)(
        decode_sources.T.reshape(-1, 128)
    )
    (grid_proj,) = call(project_kernel, [VMEM] * 2, [shape(grid_count, latent)], [], 10**9)(
        grid_latent, decode_weights
    )
    arrived = [outgoing[0]] + [along(outgoing[k], k) for k in (1, 2, 3)]
    own, chip, cross = (jnp.stack([x[part] for x in arrived]) for part in range(3))
    chip, cross, encode_lanes, mesh_lanes, grid_lanes, grid_proj = lax.optimization_barrier(
        (chip, cross, encode_lanes, mesh_lanes, grid_lanes, grid_proj)
    )
    chip, cross = swap_chip(chip), swap_cross(cross)
    source_lanes, target_lanes, incidence = encode_lanes
    edges = encode_sources.shape[0]
    (early,) = call(
        partial(early_edges_kernel, received_starts),
        [SMEM] + [VMEM] * 6,
        [shape(edges, latent)],
        [],
        2 * edges * 1024 * latent,
    )(place, source_lanes, target_lanes, own, chip, mesh_latent, encode_weights)
    mesh_now, sent = call(
        partial(late_edges_kernel, received_starts),
        [SMEM] + [VMEM] * 8,
        [shape(nodes, latent)] * 2,
        [pltpu.VMEM((edges, latent), bf16)],
        2 * edges * 512 * latent,
    )(place, source_lanes, early, cross, incidence, mesh_latent, norm_gains[0:1], encode_weights, process_weights[0])
    for step in range(STEPS):
        weights = process_weights[4 * step : 4 * step + 4]
        following = process_weights[4 * step + 4] if step + 1 < STEPS else decode_weights[0]
        around = jnp.stack([along(sent, 1), sent, along(sent, -1)])
        mesh_now, sent = edge_pass(
            halo_starts, mesh_lanes, mesh_now, around, norm_gains[1 + step : 2 + step], weights, following
        )
    band = jnp.stack([sent] + [along(sent, k) for k in (1, 2, 3)])
    chip, cross = swap_chip(band), swap_cross(band)
    (early,) = call(
        early_grid_kernel,
        [SMEM] + [VMEM] * 3,
        [shape(3 * grid_count, latent)],
        [],
        2 * 3 * grid_count * 8 * nodes * latent,
    )(place, grid_lanes, band, chip)
    (grid_out,) = call(
        late_grid_kernel,
        [SMEM] + [VMEM] * 7,
        [shape(grid_count, latent)],
        [],
        10**9,
    )(place, grid_lanes, early, cross, grid_latent, grid_proj, norm_gains[STEPS + 1 : STEPS + 2], decode_weights)
    return grid_out, mesh_now


def solution(mesh):
    rows = P(("lat", "lon"), None)
    flat = P(("lat", "lon"))
    return jax.shard_map(
        shards,
        mesh=mesh,
        in_specs=(rows, rows, P(("lat", "lon"), None, None), flat, flat, flat, flat, rows, P(), P(), P(), P()),
        out_specs=(rows, rows),
        check_vma=False,
    )
```

```python
from functools import partial

import jax
import jax.numpy as jnp
from jax import lax
from jax.experimental import pallas as pl
from jax.experimental.pallas import tpu as pltpu
from jax.sharding import PartitionSpec as P

STEPS = 2
EDGE_BLOCK = 1024
SEND_VMEM = 63
GRID_BLOCK = 1024
epsilon = 1e-05
VMEM = pl.BlockSpec(memory_space=pltpu.VMEM)
HBM = pl.BlockSpec(memory_space=pltpu.HBM)
f32, bf16, i16 = jnp.float32, jnp.bfloat16, jnp.int16


def dot(a, b):
    return jnp.dot(a, b, preferred_element_type=f32)


def silu(z):
    half = 0.5 * z
    return half + half * jnp.tanh(half)


def node_update(latent, summed, gain_row, node_weight):
    mean_square = jnp.mean(summed * summed, axis=-1, keepdims=True)
    scaled = (summed * lax.rsqrt(mean_square + epsilon) * gain_row).astype(bf16)
    return latent.astype(f32) + dot(scaled, node_weight)


def position():
    return lax.rem(lax.axis_index("lat"), 2), lax.axis_index("lon")


def send_kernel(lists, grid, weights, out0, out1, out2, out3, rows_in, weight, table, picked, wanted, sems):
    odd, lon = position()
    slots = 128
    parts = 4
    size = rows_in.shape[0] // parts
    fetch = [pltpu.make_async_copy(weights.at[0], weight, sems.at[0])]
    for n in range(parts):
        here = pl.ds(n * size, size)
        fetch.append(pltpu.make_async_copy(grid.at[here], rows_in.at[here], sems.at[1 + n]))
    for k in range(4):
        for part, side in enumerate((1, 2 - 2 * odd, 2 * odd)):
            n = 3 * k + part
            fetch.append(
                pltpu.make_async_copy(
                    lists.at[side, lax.rem(lon + k, 4)], wanted.at[pl.ds(n * slots, slots)], sems.at[1 + parts + n]
                )
            )
    for copy in fetch:
        copy.start()
    fetch[0].wait()
    for n in range(parts):
        fetch[1 + n].wait()
        here = pl.ds(n * size, size)
        table[here] = dot(rows_in[here, :], weight[...]).reshape(size, 2, 128)
    for copy in fetch[1 + parts :]:
        copy.wait()
    for k, out in enumerate((out0, out1, out2, out3)):
        for part in range(3):
            base = (3 * k + part) * slots

            @pl.loop(0, slots // 32)
            def _(i):
                rows = [table[wanted[base + i * 32 + u]] for u in range(32)]
                for u in range(32):
                    picked[base + i * 32 + u] = rows[u]

            out[part] = picked[base : base + slots].reshape(slots, 256).astype(bf16)


def lane_copies(row):
    return jnp.transpose(jnp.broadcast_to(row, (128, 128))).astype(i16)


def lanes_kernel(indices, out):
    for q in range(indices.shape[0]):
        out[q * 128 : (q + 1) * 128, :] = lane_copies(indices[q : q + 1, :])


def edge_lanes_kernel(sources, targets, source_out, target_out, incidence_out):
    lanes_kernel(sources, source_out)
    lanes_kernel(targets, target_out)
    node_ids = lax.broadcasted_iota(jnp.int32, (incidence_out.shape[0], 128), 0)
    for q in range(targets.shape[0]):
        incidence_out[:, q * 128 : (q + 1) * 128] = (node_ids == targets[q : q + 1, :]).astype(bf16)


def pointers(copies, starts, width):
    lane = lax.broadcasted_iota(jnp.int32, (1, 128), 1)
    one, zero = jnp.ones((), bf16), jnp.zeros((), bf16)
    return jnp.concatenate(
        [
            jnp.where(copies == (lane + (start + offset)).astype(i16), one, zero)
            for start in starts
            for offset in range(0, width, 128)
        ],
        1,
    )


def received_starts(width):
    odd, lon = position()
    return [[(band * 4 + lax.rem(lon + 4 - k, 4)) * width for k in range(4)] for band in (1, 2 - 2 * odd, 2 * odd)]


def halo_starts(width):
    odd, _ = position()
    return [[(band * 3 + q) * width for q in range(3)] for band in (1, 2 - 2 * odd, 2 * odd)]


def early_edges_kernel(starts, set_index, sources, targets, own, chip, latent, weights, out):
    width = own.shape[1]
    own_starts, chip_starts, _ = starts(width)
    target_proj = dot(latent[...], weights[4 * set_index + 1]).astype(bf16)
    tables = [x[...].reshape(-1, 256) for x in (own, chip)]
    size = min(EDGE_BLOCK, out.shape[0])
    for first in range(0, out.shape[0], size):
        here = slice(first, first + size)
        copies = sources[here, :]
        out[here, :] = (
            dot(pointers(targets[here, :], [0], 256), target_proj)
            + dot(pointers(copies, own_starts, width), tables[0])
            + dot(pointers(copies, chip_starts, width), tables[1])
        ).astype(bf16)


def late_edges_kernel(
    starts, set_index, stage, sources, early, cross, incidence, latent, gains, weights, following,
    latent_out, sent_out, hidden
):
    width = cross.shape[1]
    cross_starts = starts(width)[2]
    table = cross[...].reshape(-1, 256)
    size = min(EDGE_BLOCK, hidden.shape[0])
    for first in range(0, hidden.shape[0], size):
        here = slice(first, first + size)
        z = early[here, :].astype(f32) + dot(pointers(sources[here, :], cross_starts, width), table)
        hidden[here, :] = silu(z).astype(bf16)
    summed = dot(incidence[...], hidden[...])
    summed = dot(summed.astype(bf16), weights[4 * set_index + 2])
    gain = gains[stage : stage + 1, :].astype(f32)
    new = node_update(latent[...], summed, gain, weights[4 * set_index + 3]).astype(bf16)
    latent_out[...] = new
    sent_out[...] = dot(new, following[4 * (stage % STEPS)]).astype(bf16)


def own_grid_kernel(sources, own, out):
    width = own.shape[0]
    starts = received_starts(width)[0][:1]

    @pl.loop(0, out.shape[0] // EDGE_BLOCK)
    def _(j):
        here = pl.ds(pl.multiple_of(j * EDGE_BLOCK, EDGE_BLOCK), EDGE_BLOCK)
        out[here, :] = dot(pointers(sources[here, :], starts, width), own[...]).astype(bf16)


def early_grid_kernel(sources, before, own, chip, out):
    width = own.shape[1]
    own_starts, chip_starts, _ = received_starts(width)
    starts = own_starts[1:] + chip_starts
    table = jnp.concatenate([own[1:].reshape(-1, 256), chip[...].reshape(-1, 256)], 0)

    @pl.loop(0, out.shape[0] // EDGE_BLOCK)
    def _(j):
        here = pl.ds(pl.multiple_of(j * EDGE_BLOCK, EDGE_BLOCK), EDGE_BLOCK)
        found = dot(pointers(sources[here, :], starts, width), table)
        out[here, :] = (before[here, :].astype(f32) + found).astype(bf16)


def late_grid_kernel(sources, early, cross, grid, proj, gain, weights, out):
    width = cross.shape[1]
    cross_starts = received_starts(width)[2]
    table = cross[...].reshape(-1, 256)
    gains = gain[STEPS + 1 : STEPS + 2, :].astype(f32)
    count = grid.shape[0]
    @pl.loop(0, count // GRID_BLOCK)
    def _(j):
        first = pl.multiple_of(j * GRID_BLOCK, GRID_BLOCK)
        here = pl.ds(first, GRID_BLOCK)
        base = proj[here, :].astype(f32)
        hidden = jnp.zeros((GRID_BLOCK, 256), f32)
        for k in range(3):
            rows = pl.ds(pl.multiple_of(k * count + first, GRID_BLOCK), GRID_BLOCK)
            late = dot(pointers(sources[rows, :], cross_starts, width), table)
            hidden += silu(late + early[rows, :].astype(f32) + base)
        summed = dot(hidden.astype(bf16), weights[2])
        out[here, :] = node_update(grid[here, :], summed, gains, weights[3]).astype(bf16)


def project_kernel(rows, weights, out):
    out[...] = dot(rows[...], weights[1]).astype(bf16)


def shape(*dims, dtype=bf16):
    return jax.ShapeDtypeStruct(dims, dtype)


def call(kernel, specs, outs, scratch, cost, limit=20):
    return pl.pallas_call(
        kernel,
        in_specs=specs,
        out_specs=tuple(VMEM for _ in outs),
        out_shape=tuple(outs),
        scratch_shapes=scratch,
        compiler_params=pltpu.CompilerParams(vmem_limit_bytes=limit * 2**20),
        cost_estimate=pl.CostEstimate(flops=cost, bytes_accessed=2**20, transcendentals=0),
    )


def along(x, by):
    return lax.ppermute(x, "lon", [(i, (i + by) % 4) for i in range(4)])


def swap_chip(x):
    return lax.ppermute(x, "lat", [(i, i ^ 1) for i in range(32)])


def swap_cross(x):
    return lax.ppermute(x, "lat", [(i, ((i + 1) ^ 1) - 1) if 0 < i < 31 else (i, 31 - i) for i in range(32)])


def shards(
    grid_latent,
    mesh_latent,
    encode_sends,
    encode_sources,
    encode_targets,
    mesh_sources,
    mesh_targets,
    decode_sources,
    encode_weights,
    process_weights,
    decode_weights,
    norm_gains,
):
    grid_count, latent = grid_latent.shape
    nodes = mesh_latent.shape[0]

    def edge_lanes(sources, targets):
        edges = sources.shape[0]
        return call(
            edge_lanes_kernel,
            [VMEM] * 2,
            [shape(edges, 128, dtype=i16)] * 2 + [shape(nodes, edges)],
            [],
            10**9,
        )(sources.reshape(-1, 128), targets.reshape(-1, 128))

    def edge_pass(starts, stage, lanes, mesh_now, own, chip, cross):
        source_lanes, target_lanes, incidence = lanes
        edges = source_lanes.shape[0]
        rows = own.shape[0] * own.shape[1]
        weights = process_weights if stage else encode_weights
        following = process_weights if stage < STEPS else decode_weights
        set_index = stage - 1 if stage else 0
        chip, cross = swap_chip(chip), swap_cross(cross)
        (early,) = call(
            partial(early_edges_kernel, starts, set_index),
            [VMEM] * 6,
            [shape(edges, latent)],
            [],
            2 * edges * 2 * rows * latent,
        )(source_lanes, target_lanes, own, chip, mesh_now, weights)
        return call(
            partial(late_edges_kernel, starts, set_index, stage),
            [VMEM] * 8,
            [shape(nodes, latent)] * 2,
            [pltpu.VMEM((edges, latent), bf16)],
            2 * edges * rows * latent,
        )(source_lanes, early, cross, incidence, mesh_now, norm_gains, weights, following)

    outgoing = call(
        send_kernel,
        [HBM] * 3,
        [shape(3, 128, latent)] * 4,
        [
            pltpu.VMEM((grid_count, latent), bf16),
            pltpu.VMEM((latent, latent), bf16),
            pltpu.VMEM((grid_count, 2, 128), f32),
            pltpu.VMEM((1536, 2, 128), f32),
            pltpu.SMEM((1536,), jnp.int32),
            pltpu.SemaphoreType.DMA((17,)),
        ],
        10**9,
        SEND_VMEM,
    )(encode_sends, grid_latent, encode_weights)
    encode_lanes = edge_lanes(encode_sources, encode_targets)
    mesh_lanes = edge_lanes(mesh_sources, mesh_targets)
    (grid_lanes,) = call(lanes_kernel, [VMEM], [shape(3 * grid_count, 128, dtype=i16)], [], 10**9)(
        decode_sources.T.reshape(-1, 128)
    )
    (grid_proj,) = call(project_kernel, [VMEM] * 2, [shape(grid_count, latent)], [], 10**9)(
        grid_latent, decode_weights
    )
    arrived = [outgoing[0]] + [along(outgoing[k], k) for k in (1, 2, 3)]
    own, chip, cross = (jnp.stack([x[part] for x in arrived]) for part in range(3))
    chip, cross, encode_lanes, mesh_lanes, grid_lanes, grid_proj = lax.optimization_barrier(
        (chip, cross, encode_lanes, mesh_lanes, grid_lanes, grid_proj)
    )
    mesh_now, sent = edge_pass(received_starts, 0, encode_lanes, mesh_latent, own, chip, cross)
    for step in range(STEPS):
        around = jnp.stack([along(sent, 1), sent, along(sent, -1)])
        mesh_now, sent = edge_pass(halo_starts, step + 1, mesh_lanes, mesh_now, around, around, around)
    beside = [along(sent, k) for k in (1, 2, 3)]
    (before,) = call(
        own_grid_kernel,
        [VMEM] * 2,
        [shape(3 * grid_count, latent)],
        [],
        2 * 3 * grid_count * nodes * latent,
    )(grid_lanes, sent)
    band = jnp.stack([sent] + beside)
    band, before = lax.optimization_barrier((band, before))
    chip, cross = swap_chip(band), swap_cross(band)
    (early,) = call(
        early_grid_kernel,
        [VMEM] * 4,
        [shape(3 * grid_count, latent)],
        [],
        2 * 3 * grid_count * 7 * nodes * latent,
    )(grid_lanes, before, band, chip)
    (grid_out,) = call(
        late_grid_kernel,
        [VMEM] * 7,
        [shape(grid_count, latent)],
        [],
        10**9,
    )(grid_lanes, early, cross, grid_latent, grid_proj, norm_gains, decode_weights)
    return grid_out, mesh_now


def solution(mesh):
    rows = P(("lat", "lon"), None)
    flat = P(("lat", "lon"))
    return jax.shard_map(
        shards,
        mesh=mesh,
        in_specs=(rows, rows, P(("lat", "lon"), None, None), flat, flat, flat, flat, rows, P(), P(), P(), P()),
        out_specs=(rows, rows),
        check_vma=False,
    )
```

```python
from functools import partial

import jax
import jax.numpy as jnp
from jax import lax
from jax.experimental import pallas as pl
from jax.experimental.pallas import tpu as pltpu
from jax.sharding import PartitionSpec as P

STEPS = 2
EDGE_BLOCK = 1024
SEND_VMEM = 62
GRID_BLOCK = 1024
epsilon = 1e-05
VMEM = pl.BlockSpec(memory_space=pltpu.VMEM)
HBM = pl.BlockSpec(memory_space=pltpu.HBM)
f32, bf16, i16 = jnp.float32, jnp.bfloat16, jnp.int16


def dot(a, b):
    return jnp.dot(a, b, preferred_element_type=f32)


def silu(z):
    half = 0.5 * z
    return half + half * jnp.tanh(half)


def node_update(latent, summed, gain_row, node_weight):
    mean_square = jnp.mean(summed * summed, axis=-1, keepdims=True)
    scaled = (summed * lax.rsqrt(mean_square + epsilon) * gain_row).astype(bf16)
    return latent.astype(f32) + dot(scaled, node_weight)


def position():
    return lax.rem(lax.axis_index("lat"), 2), lax.axis_index("lon")


def columns():
    _, lon = position()
    step = 1 - 2 * lax.rem(lon, 2)
    return [lon] + [lax.rem(lon + by + 4, 4) for by in (step, -step, 2)]


def send_kernel(lists, grid, weights, out0, out1, out2, out3, rows_in, weight, table, picked, wanted, sems):
    odd, _ = position()
    slots = 128
    parts = 4
    size = rows_in.shape[0] // parts
    fetch = [pltpu.make_async_copy(weights.at[0], weight, sems.at[0])]
    for n in range(parts):
        here = pl.ds(n * size, size)
        fetch.append(pltpu.make_async_copy(grid.at[here], rows_in.at[here], sems.at[1 + n]))
    for k in range(4):
        for part, side in enumerate((1, 2 - 2 * odd, 2 * odd)):
            n = 3 * k + part
            fetch.append(
                pltpu.make_async_copy(
                    lists.at[side, columns()[k]], wanted.at[pl.ds(n * slots, slots)], sems.at[1 + parts + n]
                )
            )
    for copy in fetch:
        copy.start()
    fetch[0].wait()
    for n in range(parts):
        fetch[1 + n].wait()
        here = pl.ds(n * size, size)
        table[here] = dot(rows_in[here, :], weight[...]).reshape(size, 2, 128)
    for copy in fetch[1 + parts :]:
        copy.wait()
    for k, out in enumerate((out0, out1, out2, out3)):
        for part in range(3):
            base = (3 * k + part) * slots

            @pl.loop(0, slots // 32)
            def _(i):
                rows = [table[wanted[base + i * 32 + u]] for u in range(32)]
                for u in range(32):
                    picked[base + i * 32 + u] = rows[u]

            out[part] = picked[base : base + slots].reshape(slots, 256).astype(bf16)


def lane_copies(row):
    return jnp.transpose(jnp.broadcast_to(row, (128, 128))).astype(i16)


def lanes_kernel(indices, out):
    for q in range(indices.shape[0]):
        out[q * 128 : (q + 1) * 128, :] = lane_copies(indices[q : q + 1, :])


def edge_lanes_kernel(sources, targets, source_out, target_out, incidence_out):
    lanes_kernel(sources, source_out)
    lanes_kernel(targets, target_out)
    node_ids = lax.broadcasted_iota(jnp.int32, (incidence_out.shape[0], 128), 0)
    for q in range(targets.shape[0]):
        incidence_out[:, q * 128 : (q + 1) * 128] = (node_ids == targets[q : q + 1, :]).astype(bf16)


def pointers(copies, starts, width):
    lane = lax.broadcasted_iota(jnp.int32, (1, 128), 1)
    one, zero = jnp.ones((), bf16), jnp.zeros((), bf16)
    return jnp.concatenate(
        [
            jnp.where(copies == (lane + (start + offset)).astype(i16), one, zero)
            for start in starts
            for offset in range(0, width, 128)
        ],
        1,
    )


def received_starts(width):
    odd, _ = position()
    return [[(band * 4 + column) * width for column in columns()] for band in (1, 2 - 2 * odd, 2 * odd)]


def halo_starts(width):
    odd, lon = position()
    step = 1 - 2 * lax.rem(lon, 2)
    return [[(band * 3 + q) * width for q in (1 + step, 1, 1 - step)] for band in (1, 2 - 2 * odd, 2 * odd)]


def early_edges_kernel(starts, set_index, sources, targets, own, chip, latent, weights, out):
    width = own.shape[1]
    own_starts, chip_starts, _ = starts(width)
    target_proj = dot(latent[...], weights[4 * set_index + 1]).astype(bf16)
    tables = [x[...].reshape(-1, 256) for x in (own, chip)]
    size = min(EDGE_BLOCK, out.shape[0])
    for first in range(0, out.shape[0], size):
        here = slice(first, first + size)
        copies = sources[here, :]
        out[here, :] = (
            dot(pointers(targets[here, :], [0], 256), target_proj)
            + dot(pointers(copies, own_starts, width), tables[0])
            + dot(pointers(copies, chip_starts, width), tables[1])
        ).astype(bf16)


def late_edges_kernel(
    starts, set_index, stage, sources, early, cross, incidence, latent, gains, weights, following,
    latent_out, sent_out, hidden
):
    width = cross.shape[1]
    cross_starts = starts(width)[2]
    table = cross[...].reshape(-1, 256)
    size = min(EDGE_BLOCK, hidden.shape[0])
    for first in range(0, hidden.shape[0], size):
        here = slice(first, first + size)
        z = early[here, :].astype(f32) + dot(pointers(sources[here, :], cross_starts, width), table)
        hidden[here, :] = silu(z).astype(bf16)
    summed = dot(incidence[...], hidden[...])
    summed = dot(summed.astype(bf16), weights[4 * set_index + 2])
    gain = gains[stage : stage + 1, :].astype(f32)
    new = node_update(latent[...], summed, gain, weights[4 * set_index + 3]).astype(bf16)
    latent_out[...] = new
    sent_out[...] = dot(new, following[4 * (stage % STEPS)]).astype(bf16)


def own_grid_kernel(sources, own, out):
    width = own.shape[0]
    starts = received_starts(width)[0][:1]

    @pl.loop(0, out.shape[0] // EDGE_BLOCK)
    def _(j):
        here = pl.ds(pl.multiple_of(j * EDGE_BLOCK, EDGE_BLOCK), EDGE_BLOCK)
        out[here, :] = dot(pointers(sources[here, :], starts, width), own[...]).astype(bf16)


def early_grid_kernel(sources, before, own, chip, out):
    width = own.shape[1]
    own_starts, chip_starts, _ = received_starts(width)
    starts = own_starts[1:] + chip_starts
    table = jnp.concatenate([own[1:].reshape(-1, 256), chip[...].reshape(-1, 256)], 0)

    @pl.loop(0, out.shape[0] // EDGE_BLOCK)
    def _(j):
        here = pl.ds(pl.multiple_of(j * EDGE_BLOCK, EDGE_BLOCK), EDGE_BLOCK)
        found = dot(pointers(sources[here, :], starts, width), table)
        out[here, :] = (before[here, :].astype(f32) + found).astype(bf16)


def late_grid_kernel(sources, early, cross, grid, proj, gain, weights, out):
    width = cross.shape[1]
    cross_starts = received_starts(width)[2]
    table = cross[...].reshape(-1, 256)
    gains = gain[STEPS + 1 : STEPS + 2, :].astype(f32)
    count = grid.shape[0]
    @pl.loop(0, count // GRID_BLOCK)
    def _(j):
        first = pl.multiple_of(j * GRID_BLOCK, GRID_BLOCK)
        here = pl.ds(first, GRID_BLOCK)
        base = proj[here, :].astype(f32)
        hidden = jnp.zeros((GRID_BLOCK, 256), f32)
        for k in range(3):
            rows = pl.ds(pl.multiple_of(k * count + first, GRID_BLOCK), GRID_BLOCK)
            late = dot(pointers(sources[rows, :], cross_starts, width), table)
            hidden += silu(late + early[rows, :].astype(f32) + base)
        summed = dot(hidden.astype(bf16), weights[2])
        out[here, :] = node_update(grid[here, :], summed, gains, weights[3]).astype(bf16)


def project_kernel(rows, weights, out):
    out[...] = dot(rows[...], weights[1]).astype(bf16)


def shape(*dims, dtype=bf16):
    return jax.ShapeDtypeStruct(dims, dtype)


def call(kernel, specs, outs, scratch, cost, limit=20):
    return pl.pallas_call(
        kernel,
        in_specs=specs,
        out_specs=tuple(VMEM for _ in outs),
        out_shape=tuple(outs),
        scratch_shapes=scratch,
        compiler_params=pltpu.CompilerParams(vmem_limit_bytes=limit * 2**20),
        cost_estimate=pl.CostEstimate(flops=cost, bytes_accessed=2**20, transcendentals=0),
    )


def along(x, k):
    to = ((0, 1, 2, 3), (1, 0, 3, 2), (3, 2, 1, 0), (2, 3, 0, 1))[k]
    return lax.ppermute(x, "lon", list(enumerate(to)))


def swap_chip(x):
    return lax.ppermute(x, "lat", [(i, i ^ 1) for i in range(32)])


def swap_cross(x):
    return lax.ppermute(x, "lat", [(i, ((i + 1) ^ 1) - 1) if 0 < i < 31 else (i, 31 - i) for i in range(32)])


def shards(
    grid_latent,
    mesh_latent,
    encode_sends,
    encode_sources,
    encode_targets,
    mesh_sources,
    mesh_targets,
    decode_sources,
    encode_weights,
    process_weights,
    decode_weights,
    norm_gains,
):
    grid_count, latent = grid_latent.shape
    nodes = mesh_latent.shape[0]

    def edge_lanes(sources, targets):
        edges = sources.shape[0]
        return call(
            edge_lanes_kernel,
            [VMEM] * 2,
            [shape(edges, 128, dtype=i16)] * 2 + [shape(nodes, edges)],
            [],
            10**9,
        )(sources.reshape(-1, 128), targets.reshape(-1, 128))

    def edge_pass(starts, stage, lanes, mesh_now, own, chip, cross):
        source_lanes, target_lanes, incidence = lanes
        edges = source_lanes.shape[0]
        rows = own.shape[0] * own.shape[1]
        weights = process_weights if stage else encode_weights
        following = process_weights if stage < STEPS else decode_weights
        set_index = stage - 1 if stage else 0
        chip, cross = swap_chip(chip), swap_cross(cross)
        (early,) = call(
            partial(early_edges_kernel, starts, set_index),
            [VMEM] * 6,
            [shape(edges, latent)],
            [],
            2 * edges * 2 * rows * latent,
        )(source_lanes, target_lanes, own, chip, mesh_now, weights)
        return call(
            partial(late_edges_kernel, starts, set_index, stage),
            [VMEM] * 8,
            [shape(nodes, latent)] * 2,
            [pltpu.VMEM((edges, latent), bf16)],
            2 * edges * rows * latent,
        )(source_lanes, early, cross, incidence, mesh_now, norm_gains, weights, following)

    outgoing = call(
        send_kernel,
        [HBM] * 3,
        [shape(3, 128, latent)] * 4,
        [
            pltpu.VMEM((grid_count, latent), bf16),
            pltpu.VMEM((latent, latent), bf16),
            pltpu.VMEM((grid_count, 2, 128), f32),
            pltpu.VMEM((1536, 2, 128), f32),
            pltpu.SMEM((1536,), jnp.int32),
            pltpu.SemaphoreType.DMA((17,)),
        ],
        10**9,
        SEND_VMEM,
    )(encode_sends, grid_latent, encode_weights)
    encode_lanes = edge_lanes(encode_sources, encode_targets)
    mesh_lanes = edge_lanes(mesh_sources, mesh_targets)
    (grid_lanes,) = call(lanes_kernel, [VMEM], [shape(3 * grid_count, 128, dtype=i16)], [], 10**9)(
        decode_sources.T.reshape(-1, 128)
    )
    (grid_proj,) = call(project_kernel, [VMEM] * 2, [shape(grid_count, latent)], [], 10**9)(
        grid_latent, decode_weights
    )
    arrived = [outgoing[0]] + [along(outgoing[k], k) for k in (1, 2, 3)]
    own, chip, cross = (jnp.stack([x[part] for x in arrived]) for part in range(3))
    chip, cross, encode_lanes, mesh_lanes, grid_lanes, grid_proj = lax.optimization_barrier(
        (chip, cross, encode_lanes, mesh_lanes, grid_lanes, grid_proj)
    )
    mesh_now, sent = edge_pass(received_starts, 0, encode_lanes, mesh_latent, own, chip, cross)
    for step in range(STEPS):
        around = jnp.stack([along(sent, 1), sent, along(sent, 2)])
        mesh_now, sent = edge_pass(halo_starts, step + 1, mesh_lanes, mesh_now, around, around, around)
    beside = [along(sent, k) for k in (1, 2, 3)]
    (before,) = call(
        own_grid_kernel,
        [VMEM] * 2,
        [shape(3 * grid_count, latent)],
        [],
        2 * 3 * grid_count * nodes * latent,
    )(grid_lanes, sent)
    band = jnp.stack([sent] + beside)
    band, before = lax.optimization_barrier((band, before))
    chip, cross = swap_chip(band), swap_cross(band)
    (early,) = call(
        early_grid_kernel,
        [VMEM] * 4,
        [shape(3 * grid_count, latent)],
        [],
        2 * 3 * grid_count * 7 * nodes * latent,
    )(grid_lanes, before, band, chip)
    (grid_out,) = call(
        late_grid_kernel,
        [VMEM] * 7,
        [shape(grid_count, latent)],
        [],
        10**9,
    )(grid_lanes, early, cross, grid_latent, grid_proj, norm_gains, decode_weights)
    return grid_out, mesh_now


def solution(mesh):
    rows = P(("lat", "lon"), None)
    flat = P(("lat", "lon"))
    return jax.shard_map(
        shards,
        mesh=mesh,
        in_specs=(rows, rows, P(("lat", "lon"), None, None), flat, flat, flat, flat, rows, P(), P(), P(), P()),
        out_specs=(rows, rows),
        check_vma=False,
    )
```

```python
from functools import partial

import jax
import jax.numpy as jnp
from jax import lax
from jax.experimental import pallas as pl
from jax.experimental.pallas import tpu as pltpu
from jax.sharding import PartitionSpec as P

STEPS = 2
EDGE_BLOCK = 1024
SEND_VMEM = 62
GRID_BLOCK = 1024
epsilon = 1e-05
VMEM = pl.BlockSpec(memory_space=pltpu.VMEM)
HBM = pl.BlockSpec(memory_space=pltpu.HBM)
f32, bf16, i16 = jnp.float32, jnp.bfloat16, jnp.int16


def dot(a, b):
    return jnp.dot(a, b, preferred_element_type=f32)


def silu(z):
    half = 0.5 * z
    return half + half * jnp.tanh(half)


def node_update(latent, summed, gain_row, node_weight):
    mean_square = jnp.mean(summed * summed, axis=-1, keepdims=True)
    scaled = (summed * lax.rsqrt(mean_square + epsilon) * gain_row).astype(bf16)
    return latent.astype(f32) + dot(scaled, node_weight)


def position():
    return lax.rem(lax.axis_index("lat"), 2), lax.axis_index("lon")


def columns():
    _, lon = position()
    step = 1 - 2 * lax.rem(lon, 2)
    return [lon] + [lax.rem(lon + by + 4, 4) for by in (step, -step, 2)]


def send_kernel(
    lists, grid, weights, out0, out1, out2, out3, rows_in, weight, table, picked, wanted, staged, sems, out_sems
):
    odd, _ = position()
    slots = 128
    parts = 4
    size = rows_in.shape[0] // parts
    fetch = [pltpu.make_async_copy(weights.at[0], weight, sems.at[0])]
    for n in range(parts):
        here = pl.ds(n * size, size)
        fetch.append(pltpu.make_async_copy(grid.at[here], rows_in.at[here], sems.at[1 + n]))
    for k in range(4):
        for part, side in enumerate((1, 2 - 2 * odd, 2 * odd)):
            n = 3 * k + part
            fetch.append(
                pltpu.make_async_copy(
                    lists.at[side, columns()[k]], wanted.at[pl.ds(n * slots, slots)], sems.at[1 + parts + n]
                )
            )
    for copy in fetch:
        copy.start()
    fetch[0].wait()
    for n in range(parts):
        fetch[1 + n].wait()
        here = pl.ds(n * size, size)
        table[here] = dot(rows_in[here, :], weight[...]).reshape(size, 2, 128)
    for copy in fetch[1 + parts :]:
        copy.wait()
    sent = []
    for k, out in ((1, out1), (2, out2), (3, out3), (0, out0)):
        for part in range(3):
            base = (3 * k + part) * slots

            @pl.loop(0, slots // 32)
            def _(i):
                rows = [table[wanted[base + i * 32 + u]] for u in range(32)]
                for u in range(32):
                    picked[base + i * 32 + u] = rows[u]

            staged[k, part] = picked[base : base + slots].reshape(slots, 256).astype(bf16)
        sent.append(pltpu.make_async_copy(staged.at[k], out, out_sems.at[k]))
        sent[-1].start()
    for copy in sent:
        copy.wait()


def lane_copies(row):
    return jnp.transpose(jnp.broadcast_to(row, (128, 128))).astype(i16)


def lanes_kernel(indices, out):
    for q in range(indices.shape[0]):
        out[q * 128 : (q + 1) * 128, :] = lane_copies(indices[q : q + 1, :])


def edge_lanes_kernel(sources, targets, source_out, target_out, incidence_out):
    lanes_kernel(sources, source_out)
    lanes_kernel(targets, target_out)
    node_ids = lax.broadcasted_iota(jnp.int32, (incidence_out.shape[0], 128), 0)
    for q in range(targets.shape[0]):
        incidence_out[:, q * 128 : (q + 1) * 128] = (node_ids == targets[q : q + 1, :]).astype(bf16)


def pointers(copies, starts, width):
    lane = lax.broadcasted_iota(jnp.int32, (1, 128), 1)
    one, zero = jnp.ones((), bf16), jnp.zeros((), bf16)
    return jnp.concatenate(
        [
            jnp.where(copies == (lane + (start + offset)).astype(i16), one, zero)
            for start in starts
            for offset in range(0, width, 128)
        ],
        1,
    )


def received_starts(width):
    odd, _ = position()
    return [[(band * 4 + column) * width for column in columns()] for band in (1, 2 - 2 * odd, 2 * odd)]


def halo_starts(width):
    odd, lon = position()
    step = 1 - 2 * lax.rem(lon, 2)
    return [[(band * 3 + q) * width for q in (1 + step, 1, 1 - step)] for band in (1, 2 - 2 * odd, 2 * odd)]


def early_edges_kernel(starts, set_index, sources, targets, own, chip, latent, weights, out):
    width = own.shape[1]
    own_starts, chip_starts, _ = starts(width)
    target_proj = dot(latent[...], weights[4 * set_index + 1]).astype(bf16)
    tables = [x[...].reshape(-1, 256) for x in (own, chip)]
    size = min(EDGE_BLOCK, out.shape[0])
    for first in range(0, out.shape[0], size):
        here = slice(first, first + size)
        copies = sources[here, :]
        out[here, :] = (
            dot(pointers(targets[here, :], [0], 256), target_proj)
            + dot(pointers(copies, own_starts, width), tables[0])
            + dot(pointers(copies, chip_starts, width), tables[1])
        ).astype(bf16)


def late_edges_kernel(
    starts, set_index, stage, sources, early, cross, incidence, latent, gains, weights, following,
    latent_out, sent_out, hidden
):
    width = cross.shape[1]
    cross_starts = starts(width)[2]
    table = cross[...].reshape(-1, 256)
    size = min(EDGE_BLOCK, hidden.shape[0])
    for first in range(0, hidden.shape[0], size):
        here = slice(first, first + size)
        z = early[here, :].astype(f32) + dot(pointers(sources[here, :], cross_starts, width), table)
        hidden[here, :] = silu(z).astype(bf16)
    summed = dot(incidence[...], hidden[...])
    summed = dot(summed.astype(bf16), weights[4 * set_index + 2])
    gain = gains[stage : stage + 1, :].astype(f32)
    new = node_update(latent[...], summed, gain, weights[4 * set_index + 3]).astype(bf16)
    latent_out[...] = new
    sent_out[...] = dot(new, following[4 * (stage % STEPS)]).astype(bf16)


def own_grid_kernel(sources, own, latent, out, latent_out):
    width = own.shape[0]
    starts = received_starts(width)[0][:1]
    latent_out[...] = latent[...]

    @pl.loop(0, out.shape[0] // EDGE_BLOCK)
    def _(j):
        here = pl.ds(pl.multiple_of(j * EDGE_BLOCK, EDGE_BLOCK), EDGE_BLOCK)
        out[here, :] = dot(pointers(sources[here, :], starts, width), own[...]).astype(bf16)


def early_grid_kernel(sources, before, own, chip, out):
    width = own.shape[1]
    own_starts, chip_starts, _ = received_starts(width)
    starts = own_starts[1:] + chip_starts
    table = jnp.concatenate([own[1:].reshape(-1, 256), chip[...].reshape(-1, 256)], 0)

    @pl.loop(0, out.shape[0] // EDGE_BLOCK)
    def _(j):
        here = pl.ds(pl.multiple_of(j * EDGE_BLOCK, EDGE_BLOCK), EDGE_BLOCK)
        found = dot(pointers(sources[here, :], starts, width), table)
        out[here, :] = (before[here, :].astype(f32) + found).astype(bf16)


def late_grid_kernel(sources, early, cross, grid, proj, gain, weights, out, staged, sems):
    width = cross.shape[1]
    cross_starts = received_starts(width)[2]
    table = cross[...].reshape(-1, 256)
    gains = gain[STEPS + 1 : STEPS + 2, :].astype(f32)
    count = grid.shape[0]
    @pl.loop(0, count // GRID_BLOCK)
    def _(j):
        first = pl.multiple_of(j * GRID_BLOCK, GRID_BLOCK)
        here = pl.ds(first, GRID_BLOCK)
        base = proj[here, :].astype(f32)
        hidden = jnp.zeros((GRID_BLOCK, 256), f32)
        for k in range(3):
            rows = pl.ds(pl.multiple_of(k * count + first, GRID_BLOCK), GRID_BLOCK)
            late = dot(pointers(sources[rows, :], cross_starts, width), table)
            hidden += silu(late + early[rows, :].astype(f32) + base)
        summed = dot(hidden.astype(bf16), weights[2])
        staged[here, :] = node_update(grid[here, :], summed, gains, weights[3]).astype(bf16)
        pltpu.make_async_copy(staged.at[here], out.at[here], sems.at[j]).start()

    for j in range(count // GRID_BLOCK):
        here = pl.ds(j * GRID_BLOCK, GRID_BLOCK)
        pltpu.make_async_copy(staged.at[here], out.at[here], sems.at[j]).wait()


def project_kernel(rows, weights, out):
    out[...] = dot(rows[...], weights[1]).astype(bf16)


def shape(*dims, dtype=bf16):
    return jax.ShapeDtypeStruct(dims, dtype)


def call(kernel, specs, outs, scratch, cost, limit=20, out_space=VMEM):
    return pl.pallas_call(
        kernel,
        in_specs=specs,
        out_specs=tuple(out_space for _ in outs),
        out_shape=tuple(outs),
        scratch_shapes=scratch,
        compiler_params=pltpu.CompilerParams(vmem_limit_bytes=limit * 2**20),
        cost_estimate=pl.CostEstimate(flops=cost, bytes_accessed=2**20, transcendentals=0),
    )


def along(x, k):
    to = ((0, 1, 2, 3), (1, 0, 3, 2), (3, 2, 1, 0), (2, 3, 0, 1))[k]
    return lax.ppermute(x, "lon", list(enumerate(to)))


def swap_chip(x):
    return lax.ppermute(x, "lat", [(i, i ^ 1) for i in range(32)])


def swap_cross(x):
    return lax.ppermute(x, "lat", [(i, ((i + 1) ^ 1) - 1) if 0 < i < 31 else (i, 31 - i) for i in range(32)])


def shards(
    grid_latent,
    mesh_latent,
    encode_sends,
    encode_sources,
    encode_targets,
    mesh_sources,
    mesh_targets,
    decode_sources,
    encode_weights,
    process_weights,
    decode_weights,
    norm_gains,
):
    grid_count, latent = grid_latent.shape
    nodes = mesh_latent.shape[0]

    def edge_lanes(sources, targets):
        edges = sources.shape[0]
        return call(
            edge_lanes_kernel,
            [VMEM] * 2,
            [shape(edges, 128, dtype=i16)] * 2 + [shape(nodes, edges)],
            [],
            10**9,
        )(sources.reshape(-1, 128), targets.reshape(-1, 128))

    def edge_pass(starts, stage, lanes, mesh_now, own, chip, cross):
        source_lanes, target_lanes, incidence = lanes
        edges = source_lanes.shape[0]
        rows = own.shape[0] * own.shape[1]
        weights = process_weights if stage else encode_weights
        following = process_weights if stage < STEPS else decode_weights
        set_index = stage - 1 if stage else 0
        chip, cross = swap_chip(chip), swap_cross(cross)
        (early,) = call(
            partial(early_edges_kernel, starts, set_index),
            [VMEM] * 6,
            [shape(edges, latent)],
            [],
            2 * edges * 2 * rows * latent,
        )(source_lanes, target_lanes, own, chip, mesh_now, weights)
        return call(
            partial(late_edges_kernel, starts, set_index, stage),
            [VMEM] * 8,
            [shape(nodes, latent)] * 2,
            [pltpu.VMEM((edges, latent), bf16)],
            2 * edges * rows * latent,
        )(source_lanes, early, cross, incidence, mesh_now, norm_gains, weights, following)

    outgoing = call(
        send_kernel,
        [HBM] * 3,
        [shape(3, 128, latent)] * 4,
        [
            pltpu.VMEM((grid_count, latent), bf16),
            pltpu.VMEM((latent, latent), bf16),
            pltpu.VMEM((grid_count, 2, 128), f32),
            pltpu.VMEM((1536, 2, 128), f32),
            pltpu.SMEM((1536,), jnp.int32),
            pltpu.VMEM((4, 3, 128, latent), bf16),
            pltpu.SemaphoreType.DMA((17,)),
            pltpu.SemaphoreType.DMA((4,)),
        ],
        10**9,
        SEND_VMEM,
        HBM,
    )(encode_sends, grid_latent, encode_weights)
    encode_lanes = edge_lanes(encode_sources, encode_targets)
    mesh_lanes = edge_lanes(mesh_sources, mesh_targets)
    (grid_lanes,) = call(lanes_kernel, [VMEM], [shape(3 * grid_count, 128, dtype=i16)], [], 10**9)(
        decode_sources.T.reshape(-1, 128)
    )
    (grid_proj,) = call(project_kernel, [VMEM] * 2, [shape(grid_count, latent)], [], 10**9)(
        grid_latent, decode_weights
    )
    arrived = [outgoing[0]] + [along(outgoing[k], k) for k in (1, 2, 3)]
    own, chip, cross = (jnp.stack([x[part] for x in arrived]) for part in range(3))
    chip, cross, encode_lanes, mesh_lanes, grid_lanes, grid_proj = lax.optimization_barrier(
        (chip, cross, encode_lanes, mesh_lanes, grid_lanes, grid_proj)
    )
    mesh_now, sent = edge_pass(received_starts, 0, encode_lanes, mesh_latent, own, chip, cross)
    for step in range(STEPS):
        around = jnp.stack([along(sent, 1), sent, along(sent, 2)])
        mesh_now, sent = edge_pass(halo_starts, step + 1, mesh_lanes, mesh_now, around, around, around)
    beside = [along(sent, k) for k in (1, 2, 3)]
    before, mesh_out = call(
        own_grid_kernel,
        [VMEM] * 3,
        [shape(3 * grid_count, latent), shape(nodes, latent)],
        [],
        2 * 3 * grid_count * nodes * latent,
    )(grid_lanes, sent, mesh_now)
    band = jnp.stack([sent] + beside)
    band, before = lax.optimization_barrier((band, before))
    chip, cross = swap_chip(band), swap_cross(band)
    (early,) = call(
        early_grid_kernel,
        [VMEM] * 4,
        [shape(3 * grid_count, latent)],
        [],
        2 * 3 * grid_count * 7 * nodes * latent,
    )(grid_lanes, before, band, chip)
    (grid_out,) = call(
        late_grid_kernel,
        [VMEM] * 7,
        [shape(grid_count, latent)],
        [pltpu.VMEM((grid_count, latent), bf16), pltpu.SemaphoreType.DMA((grid_count // GRID_BLOCK,))],
        10**9,
        20,
        HBM,
    )(grid_lanes, early, cross, grid_latent, grid_proj, norm_gains, decode_weights)
    return grid_out, mesh_out


def solution(mesh):
    rows = P(("lat", "lon"), None)
    flat = P(("lat", "lon"))
    return jax.shard_map(
        shards,
        mesh=mesh,
        in_specs=(rows, rows, P(("lat", "lon"), None, None), flat, flat, flat, flat, rows, P(), P(), P(), P()),
        out_specs=(rows, rows),
        check_vma=False,
    )
```

```python
from functools import partial

import jax
import jax.numpy as jnp
from jax import lax
from jax.experimental import pallas as pl
from jax.experimental.pallas import tpu as pltpu
from jax.sharding import PartitionSpec as P

STEPS = 2
EDGE_BLOCK = 1024
SEND_VMEM = 62
GRID_BLOCK = 1024
epsilon = 1e-05
VMEM = pl.BlockSpec(memory_space=pltpu.VMEM)
HBM = pl.BlockSpec(memory_space=pltpu.HBM)
f32, bf16, i16 = jnp.float32, jnp.bfloat16, jnp.int16


def dot(a, b):
    return jnp.dot(a, b, preferred_element_type=f32)


def silu(z):
    half = 0.5 * z
    return half + half * jnp.tanh(half)


def node_update(latent, summed, gain_row, node_weight):
    mean_square = jnp.mean(summed * summed, axis=-1, keepdims=True)
    scaled = (summed * lax.rsqrt(mean_square + epsilon) * gain_row).astype(bf16)
    return latent.astype(f32) + dot(scaled, node_weight)


def position():
    return lax.rem(lax.axis_index("lat"), 2), lax.axis_index("lon")


def columns():
    _, lon = position()
    step = 1 - 2 * lax.rem(lon, 2)
    return [lon] + [lax.rem(lon + by + 4, 4) for by in (step, -step, 2)]


def send_kernel(
    lists, grid, weights, out0, out1, out2, out3, rows_in, weight, table, picked, wanted, staged, sems, out_sems
):
    odd, _ = position()
    slots = 128
    parts = 4
    size = rows_in.shape[0] // parts
    fetch = [pltpu.make_async_copy(weights.at[0], weight, sems.at[0])]
    for n in range(parts):
        here = pl.ds(n * size, size)
        fetch.append(pltpu.make_async_copy(grid.at[here], rows_in.at[here], sems.at[1 + n]))
    for k in range(4):
        for part, side in enumerate((1, 2 - 2 * odd, 2 * odd)):
            n = 3 * k + part
            fetch.append(
                pltpu.make_async_copy(
                    lists.at[side, columns()[k]], wanted.at[pl.ds(n * slots, slots)], sems.at[1 + parts + n]
                )
            )
    for copy in fetch:
        copy.start()
    fetch[0].wait()
    for n in range(parts):
        fetch[1 + n].wait()
        here = pl.ds(n * size, size)
        table[here] = dot(rows_in[here, :], weight[...]).reshape(size, 2, 128)
    for copy in fetch[1 + parts :]:
        copy.wait()
    sent = []
    for k, out in ((1, out1), (2, out2), (3, out3), (0, out0)):
        for part in range(3):
            base = (3 * k + part) * slots

            for first in range(base, base + slots, 32):
                rows = [table[wanted[first + u]] for u in range(32)]
                for u in range(32):
                    picked[first + u] = rows[u]

            staged[k, part] = picked[base : base + slots].reshape(slots, 256).astype(bf16)
        sent.append(pltpu.make_async_copy(staged.at[k], out, out_sems.at[k]))
        sent[-1].start()
    for copy in sent:
        copy.wait()


def lane_copies(row):
    return jnp.transpose(jnp.broadcast_to(row, (128, 128))).astype(i16)


def lanes_kernel(indices, out):
    for q in range(indices.shape[0]):
        out[q * 128 : (q + 1) * 128, :] = lane_copies(indices[q : q + 1, :])


def edge_lanes_kernel(sources, targets, source_out, target_out, incidence_out):
    lanes_kernel(sources, source_out)
    lanes_kernel(targets, target_out)
    node_ids = lax.broadcasted_iota(jnp.int32, (incidence_out.shape[0], 128), 0)
    for q in range(targets.shape[0]):
        incidence_out[:, q * 128 : (q + 1) * 128] = (node_ids == targets[q : q + 1, :]).astype(bf16)


def pointers(copies, starts, width):
    lane = lax.broadcasted_iota(jnp.int32, (1, 128), 1)
    one, zero = jnp.ones((), bf16), jnp.zeros((), bf16)
    return jnp.concatenate(
        [
            jnp.where(copies == (lane + (start + offset)).astype(i16), one, zero)
            for start in starts
            for offset in range(0, width, 128)
        ],
        1,
    )


def received_starts(width):
    odd, _ = position()
    return [[(band * 4 + column) * width for column in columns()] for band in (1, 2 - 2 * odd, 2 * odd)]


def halo_starts(width):
    odd, lon = position()
    step = 1 - 2 * lax.rem(lon, 2)
    return [[(band * 3 + q) * width for q in (1 + step, 1, 1 - step)] for band in (1, 2 - 2 * odd, 2 * odd)]


def early_edges_kernel(starts, set_index, sources, targets, own, chip, latent, weights, out):
    width = own.shape[1]
    own_starts, chip_starts, _ = starts(width)
    target_proj = dot(latent[...], weights[4 * set_index + 1]).astype(bf16)
    tables = [x[...].reshape(-1, 256) for x in (own, chip)]
    size = min(EDGE_BLOCK, out.shape[0])
    for first in range(0, out.shape[0], size):
        here = slice(first, first + size)
        copies = sources[here, :]
        out[here, :] = (
            dot(pointers(targets[here, :], [0], 256), target_proj)
            + dot(pointers(copies, own_starts, width), tables[0])
            + dot(pointers(copies, chip_starts, width), tables[1])
        ).astype(bf16)


def late_edges_kernel(
    starts, set_index, stage, sources, early, cross, incidence, latent, gains, weights, following,
    latent_out, sent_out, hidden
):
    width = cross.shape[1]
    cross_starts = starts(width)[2]
    table = cross[...].reshape(-1, 256)
    size = min(EDGE_BLOCK, hidden.shape[0])
    for first in range(0, hidden.shape[0], size):
        here = slice(first, first + size)
        z = early[here, :].astype(f32) + dot(pointers(sources[here, :], cross_starts, width), table)
        hidden[here, :] = silu(z).astype(bf16)
    summed = dot(incidence[...], hidden[...])
    summed = dot(summed.astype(bf16), weights[4 * set_index + 2])
    gain = gains[stage : stage + 1, :].astype(f32)
    new = node_update(latent[...], summed, gain, weights[4 * set_index + 3]).astype(bf16)
    latent_out[...] = new
    sent_out[...] = dot(new, following[4 * (stage % STEPS)]).astype(bf16)


def own_grid_kernel(sources, own, proj, latent, out, latent_out):
    width = own.shape[0]
    starts = received_starts(width)[0][:1]
    latent_out[...] = latent[...]

    @pl.loop(0, out.shape[0] // EDGE_BLOCK)
    def _(j):
        here = pl.ds(pl.multiple_of(j * EDGE_BLOCK, EDGE_BLOCK), EDGE_BLOCK)
        first = lax.rem(j, proj.shape[0] // EDGE_BLOCK) * EDGE_BLOCK
        base = proj[pl.ds(pl.multiple_of(first, EDGE_BLOCK), EDGE_BLOCK), :].astype(f32)
        out[here, :] = (base + dot(pointers(sources[here, :], starts, width), own[...])).astype(bf16)


def early_grid_kernel(sources, before, own, chip, out):
    width = own.shape[1]
    own_starts, chip_starts, _ = received_starts(width)
    starts = own_starts[1:] + chip_starts
    table = jnp.concatenate([own[1:].reshape(-1, 256), chip[...].reshape(-1, 256)], 0)

    @pl.loop(0, out.shape[0] // EDGE_BLOCK)
    def _(j):
        here = pl.ds(pl.multiple_of(j * EDGE_BLOCK, EDGE_BLOCK), EDGE_BLOCK)
        found = dot(pointers(sources[here, :], starts, width), table)
        out[here, :] = (before[here, :].astype(f32) + found).astype(bf16)


def late_grid_kernel(sources, early, cross, grid, gain, weights, out, staged, sems):
    width = cross.shape[1]
    cross_starts = received_starts(width)[2]
    table = cross[...].reshape(-1, 256)
    gains = gain[STEPS + 1 : STEPS + 2, :].astype(f32)
    count = grid.shape[0]
    @pl.loop(0, count // GRID_BLOCK)
    def _(j):
        first = pl.multiple_of(j * GRID_BLOCK, GRID_BLOCK)
        here = pl.ds(first, GRID_BLOCK)
        hidden = jnp.zeros((GRID_BLOCK, 256), f32)
        for k in range(3):
            rows = pl.ds(pl.multiple_of(k * count + first, GRID_BLOCK), GRID_BLOCK)
            late = dot(pointers(sources[rows, :], cross_starts, width), table)
            hidden += silu(late + early[rows, :].astype(f32))
        summed = dot(hidden.astype(bf16), weights[2])
        staged[here, :] = node_update(grid[here, :], summed, gains, weights[3]).astype(bf16)
        pltpu.make_async_copy(staged.at[here], out.at[here], sems.at[j]).start()

    for j in range(count // GRID_BLOCK):
        here = pl.ds(j * GRID_BLOCK, GRID_BLOCK)
        pltpu.make_async_copy(staged.at[here], out.at[here], sems.at[j]).wait()


def project_kernel(rows, weights, out):
    out[...] = dot(rows[...], weights[1]).astype(bf16)


def shape(*dims, dtype=bf16):
    return jax.ShapeDtypeStruct(dims, dtype)


def call(kernel, specs, outs, scratch, cost, limit=20, out_space=VMEM):
    return pl.pallas_call(
        kernel,
        in_specs=specs,
        out_specs=tuple(out_space for _ in outs),
        out_shape=tuple(outs),
        scratch_shapes=scratch,
        compiler_params=pltpu.CompilerParams(vmem_limit_bytes=limit * 2**20),
        cost_estimate=pl.CostEstimate(flops=cost, bytes_accessed=2**20, transcendentals=0),
    )


def along(x, k):
    to = ((0, 1, 2, 3), (1, 0, 3, 2), (3, 2, 1, 0), (2, 3, 0, 1))[k]
    return lax.ppermute(x, "lon", list(enumerate(to)))


def swap_chip(x):
    return lax.ppermute(x, "lat", [(i, i ^ 1) for i in range(32)])


def swap_cross(x):
    return lax.ppermute(x, "lat", [(i, ((i + 1) ^ 1) - 1) if 0 < i < 31 else (i, 31 - i) for i in range(32)])


def shards(
    grid_latent,
    mesh_latent,
    encode_sends,
    encode_sources,
    encode_targets,
    mesh_sources,
    mesh_targets,
    decode_sources,
    encode_weights,
    process_weights,
    decode_weights,
    norm_gains,
):
    grid_count, latent = grid_latent.shape
    nodes = mesh_latent.shape[0]

    def edge_lanes(sources, targets):
        edges = sources.shape[0]
        return call(
            edge_lanes_kernel,
            [VMEM] * 2,
            [shape(edges, 128, dtype=i16)] * 2 + [shape(nodes, edges)],
            [],
            10**9,
        )(sources.reshape(-1, 128), targets.reshape(-1, 128))

    def edge_pass(starts, stage, lanes, mesh_now, own, chip, cross):
        source_lanes, target_lanes, incidence = lanes
        edges = source_lanes.shape[0]
        rows = own.shape[0] * own.shape[1]
        weights = process_weights if stage else encode_weights
        following = process_weights if stage < STEPS else decode_weights
        set_index = stage - 1 if stage else 0
        chip, cross = swap_chip(chip), swap_cross(cross)
        (early,) = call(
            partial(early_edges_kernel, starts, set_index),
            [VMEM] * 6,
            [shape(edges, latent)],
            [],
            2 * edges * 2 * rows * latent,
        )(source_lanes, target_lanes, own, chip, mesh_now, weights)
        return call(
            partial(late_edges_kernel, starts, set_index, stage),
            [VMEM] * 8,
            [shape(nodes, latent)] * 2,
            [pltpu.VMEM((edges, latent), bf16)],
            2 * edges * rows * latent,
        )(source_lanes, early, cross, incidence, mesh_now, norm_gains, weights, following)

    outgoing = call(
        send_kernel,
        [HBM] * 3,
        [shape(3, 128, latent)] * 4,
        [
            pltpu.VMEM((grid_count, latent), bf16),
            pltpu.VMEM((latent, latent), bf16),
            pltpu.VMEM((grid_count, 2, 128), f32),
            pltpu.VMEM((1536, 2, 128), f32),
            pltpu.SMEM((1536,), jnp.int32),
            pltpu.VMEM((4, 3, 128, latent), bf16),
            pltpu.SemaphoreType.DMA((17,)),
            pltpu.SemaphoreType.DMA((4,)),
        ],
        10**9,
        SEND_VMEM,
        HBM,
    )(encode_sends, grid_latent, encode_weights)
    encode_lanes = edge_lanes(encode_sources, encode_targets)
    mesh_lanes = edge_lanes(mesh_sources, mesh_targets)
    (grid_lanes,) = call(lanes_kernel, [VMEM], [shape(3 * grid_count, 128, dtype=i16)], [], 10**9)(
        decode_sources.T.reshape(-1, 128)
    )
    (grid_proj,) = call(project_kernel, [VMEM] * 2, [shape(grid_count, latent)], [], 10**9)(
        grid_latent, decode_weights
    )
    arrived = [outgoing[0]] + [along(outgoing[k], k) for k in (1, 2, 3)]
    own, chip, cross = (jnp.stack([x[part] for x in arrived]) for part in range(3))
    chip, cross, encode_lanes, mesh_lanes, grid_lanes, grid_proj = lax.optimization_barrier(
        (chip, cross, encode_lanes, mesh_lanes, grid_lanes, grid_proj)
    )
    mesh_now, sent = edge_pass(received_starts, 0, encode_lanes, mesh_latent, own, chip, cross)
    for step in range(STEPS):
        around = jnp.stack([along(sent, 1), sent, along(sent, 2)])
        mesh_now, sent = edge_pass(halo_starts, step + 1, mesh_lanes, mesh_now, around, around, around)
    beside = [along(sent, k) for k in (1, 2, 3)]
    before, mesh_out = call(
        own_grid_kernel,
        [VMEM] * 4,
        [shape(3 * grid_count, latent), shape(nodes, latent)],
        [],
        2 * 3 * grid_count * nodes * latent,
    )(grid_lanes, sent, grid_proj, mesh_now)
    band = jnp.stack([sent] + beside)
    band, before = lax.optimization_barrier((band, before))
    chip, cross = swap_chip(band), swap_cross(band)
    (early,) = call(
        early_grid_kernel,
        [VMEM] * 4,
        [shape(3 * grid_count, latent)],
        [],
        2 * 3 * grid_count * 7 * nodes * latent,
    )(grid_lanes, before, band, chip)
    (grid_out,) = call(
        late_grid_kernel,
        [VMEM] * 6,
        [shape(grid_count, latent)],
        [pltpu.VMEM((grid_count, latent), bf16), pltpu.SemaphoreType.DMA((grid_count // GRID_BLOCK,))],
        10**9,
        20,
        HBM,
    )(grid_lanes, early, cross, grid_latent, norm_gains, decode_weights)
    return grid_out, mesh_out


def solution(mesh):
    rows = P(("lat", "lon"), None)
    flat = P(("lat", "lon"))
    return jax.shard_map(
        shards,
        mesh=mesh,
        in_specs=(rows, rows, P(("lat", "lon"), None, None), flat, flat, flat, flat, rows, P(), P(), P(), P()),
        out_specs=(rows, rows),
        check_vma=False,
    )
```
